32 devices in a mesh: ens: 2 (over x), gx: 16 (over z, y, core).
Axes of the slice: x: 2, y: 2, z: 4, core: 2. Of those that a mesh axis runs over, the one named last changes fastest.
Arguments:
- ocean_vel: float32 [4, 1024, 128], P('ens', 'gx'), parts along dimension 0, may hold values from -3 to 3
- wind_stress: float32 [4, 1024, 128], P('ens', 'gx'), parts along dimension 0, may hold values from -3 to 3
- ice_area: float32 [10, 1024, 128], P('ens', 'gx'), parts along dimension 0, may hold values from 0.16 to 0.2
- ice_thick: float32 [10, 1024, 128], P('ens', 'gx'), parts along dimension 0, may hold values from 0.3 to 4
- block_mask: int32 [512], P(('ens', 'gx')), parts along dimension 0, may hold values 0 or 1
- temp: float32 [32, 1024, 128], P('ens', 'gx'), parts along dimension 0, may hold values from -6 to 6
- kappa: float32 [30, 1024, 128], P('ens', 'gx'), parts along dimension 0, may hold values from 0.1 to 10
Outputs:
- mixed_temp: float32 [32, 1024, 128], P('ens', 'gx'), parts along dimension 0
- ice_velocity: float32 [4, 1024, 128], P('ens', 'gx'), parts along dimension 0
- ice_stress: float32 [4, 1024, 128], P('ens', 'gx'), parts along dimension 0
The draws below stay inside these ranges and needn't reach their ends.
There are 2 independent parts, one for each index of `ens`. The reference program is written for one: setup_inputs(seed, part) draws one part's arguments, and reference() takes and returns one part's arrays. A program takes and returns all parts, laid end to end along the dimension named above; each array names one. Nothing has to cross between parts.
All inputs are finite; a program needn't handle non-finite values. No bound on the sum of `block_mask` on one device may be relied on, other than what follows from the above.
Results may differ from the reference program's by a relative error of at most 0.00002.
Values sent between devices are 32-bit elements; how exact they have to be, the bound alone decides.
A program may use at most 64 MiB of HBM per device.

```python
import math
import jax
import jax.numpy as jnp
from jax import lax

CAT = 5
BX = 4
NY = 128
NZ = 16
ITERS = 10
NBLK = 256
NX = 1024


def touch_ends(entries, key, least, high):
    place = [jax.random.randint(jax.random.fold_in(key, axis), (), 0, length) for axis, length in enumerate(entries.shape)]
    widest = entries.shape.index(max(entries.shape))
    neighbour = place[:widest] + [(place[widest] + 1) % entries.shape[widest]] + place[widest + 1:]
    return entries.at[tuple(place)].set(least).at[tuple(neighbour)].set(high)


def steps_of(stream_key, extent, split, low, high):
    factor_of = 1.0
    for dim, parts in split:
        steps = jax.random.uniform(jax.random.fold_in(jax.random.fold_in(stream_key, 6), dim), (parts,), jnp.float32, low / len(split), high / len(split))
        factor_of = factor_of * jnp.repeat(jnp.exp(steps), extent[dim] // parts).reshape((-1,) + (1,) * (len(extent) - 1 - dim))
    return factor_of


def bell_draw(rng, shape, width, reach, pieces=(), dtype=jnp.bfloat16):
    values = width * jax.random.normal(rng, shape, jnp.float32)
    if pieces:
        values = values * steps_of(rng, shape, pieces, -0.22, 0.18)
    return jnp.clip(values, -reach, reach).astype(dtype)


def setup_inputs(seed: int = 0, part: int = 0) -> dict:
    keys = jax.random.split(jax.random.key(seed), 8)
    part_splits = jax.random.split(jax.random.fold_in(keys[7], part), 8)
    return {
        "ocean_vel": bell_draw(part_splits[0], (2, NX, NY), 0.5, 3.0, ((1, 16),), jnp.float32),
        "wind_stress": bell_draw(part_splits[1], (2, NX, NY), 0.5, 3.0, ((1, 16),), jnp.float32),
        "ice_area": jnp.clip(0.16 + 0.040000007 * jax.random.uniform(part_splits[2], (CAT, NX, NY), jnp.float32) ** steps_of(part_splits[2], (CAT, NX, NY), ((1, 16),), -0.2, 0.2), 0.16, 0.2),
        "ice_thick": jnp.clip(jnp.exp(math.log(4.0) - 2.5902671 * jax.random.uniform(part_splits[3], (CAT, NX, NY), jnp.float32) ** steps_of(part_splits[3], (CAT, NX, NY), ((1, 16),), -0.2, 0.2)), 0.3, 4.0),
        "block_mask": touch_ends((jax.random.randint(part_splits[4], (NBLK,), 0, 4) < 3).astype(jnp.int32), jax.random.fold_in(part_splits[4], 1), 0, 1),
        "temp": bell_draw(part_splits[5], (NZ, NX, NY), 1.0, 6.0, ((1, 16),), jnp.float32),
        "kappa": jnp.clip(jnp.exp(math.log(10.0) - 4.6051702 * jax.random.uniform(part_splits[6], (NZ - 1, NX, NY), jnp.float32) ** steps_of(part_splits[6], (NZ - 1, NX, NY), ((1, 16),), -0.2, 0.2)), 0.1, 10.0),
    }


strength_coef = 27.5
hardening = 20.0
delta_floor = 0.01
relax_step = 0.5
water_drag = 1.0

def strength_of(areas, thicks):
    total = lax.optimization_barrier(jnp.sum(areas, 0))
    return (total, strength_coef * lax.optimization_barrier(jnp.sum(areas * thicks, 0)) * jnp.exp(-hardening * (1.0 - total)))

def column_mixing(temp, kappa, source):
    levels = temp.shape[0]
    factors = []
    partial_sol = []
    for level in range(levels):
        k_above = kappa[level - 1] if level > 0 else jnp.zeros_like(temp[0])
        k_below = kappa[level] if level < levels - 1 else jnp.zeros_like(temp[0])
        target = temp[0] + source if level == 0 else temp[level]
        diagonal = 1.0 + k_above + k_below
        if level == 0:
            pivot = diagonal
            solved = target / pivot
        else:
            pivot = diagonal + k_above * factors[-1]
            solved = (target + k_above * partial_sol[-1]) / pivot
        factors.append(-k_below / pivot)
        partial_sol.append(solved)
    result = [partial_sol[-1]]
    for level in range(levels - 2, -1, -1):
        result.append(partial_sol[level] - factors[level] * result[-1])
    return jnp.stack(result[::-1], 0)

def relax_global(velocity, strength, forcing, ocean, weights):
    eastern = jnp.roll(velocity, -1, axis=1)
    western = jnp.roll(velocity, 1, axis=1)
    folded = -velocity[:, ::-1, -1:]
    northern = jnp.concatenate([velocity[:, :, 1:], folded], -1)
    southern = jnp.concatenate([jnp.zeros_like(velocity[:, :, :1]), velocity[:, :, :-1]], -1)
    du_x = 0.5 * (eastern[0] - western[0])
    dv_y = 0.5 * (northern[1] - southern[1])
    du_y = 0.5 * (northern[0] - southern[0])
    dv_x = 0.5 * (eastern[1] - western[1])
    delta = jnp.sqrt((du_x + dv_y) ** 2 + 4.0 * ((du_x - dv_y) ** 2 + (du_y + dv_x) ** 2) + delta_floor)
    viscous = strength / (2.0 * delta)
    neighbour_sum = eastern + western + northern + southern
    return weights * (velocity + relax_step * (viscous * neighbour_sum + forcing + water_drag * ocean)) / (1.0 + relax_step * (4.0 * viscous + water_drag))

def reference(ocean_vel, wind_stress, ice_area, ice_thick, block_mask, temp, kappa):
    weights = jnp.repeat(block_mask.astype(jnp.float32), BX)[:, None]
    total, strength = strength_of(ice_area, ice_thick)
    velocity = ocean_vel * weights
    for count in range(ITERS):
        velocity = relax_global(velocity, strength, wind_stress, ocean_vel, weights)
    stress = water_drag * total * (velocity - ocean_vel) * weights
    source = stress[0] * ocean_vel[0] + stress[1] * ocean_vel[1]
    mixed = column_mixing(temp, kappa, source)
    return (mixed, velocity, stress)
```

```python
import functools

import jax
import jax.numpy as jnp
from jax import lax
from jax.experimental import pallas as pl
from jax.experimental.pallas import tpu as pltpu
from jax.sharding import PartitionSpec as P

ITERS = 10
HALO = 16
FIELDS = 5
MESH = pl.DeviceIdType.MESH
HIGH = lax.Precision.HIGHEST


def advance(u, v, eastern, western, northern, southern, fu, fv, half_strength):
    (eu, ev), (wu, wv), (nu, nv), (su, sv) = eastern, western, northern, southern
    du_x = eu - wu
    dv_y = nv - sv
    shear = (nu - su) + (ev - wv)
    plus = du_x + dv_y
    minus = du_x - dv_y
    squared = plus * plus + (4.0 * (minus * minus + shear * shear) + 0.04)
    half_zeta = half_strength * lax.rsqrt(squared)
    scale = 1.0 / (1.5 + 4.0 * half_zeta)
    new_u = (u + half_zeta * ((eu + wu) + (nu + su)) + fu) * scale
    new_v = (v + half_zeta * ((ev + wv) + (nv + sv)) + fv) * scale
    return new_u, new_v


def kernel(
    slots, mask, ocean_hbm, wind_hbm, area_hbm, thick_hbm, temp_hbm, kappa_hbm,
    mixed_hbm, velocity_hbm, stress_hbm,
    ocean, wind, area, thick, temp, kappa, fields, strips, mirrored, arrived,
    total_ref, weight_ref, first_ref, rows_ref, velocity, stress,
    in_sem, out_sem, send_sem, recv_sem,
):
    n = ocean.shape[1]
    levels = temp.shape[0]
    width = n // mask.shape[0]
    ens, here = lax.axis_index("ens"), lax.axis_index("gx")
    east = lax.rem(here + 1, slots)
    west = lax.rem(here + slots - 1, slots)
    partner = slots - 1 - here
    partner_east = lax.rem(partner + 1, slots)
    partner_west = lax.rem(partner + slots - 1, slots)

    loads = [
        pltpu.make_async_copy(src, dst, in_sem.at[k])
        for k, (src, dst) in enumerate([
            (area_hbm, area), (thick_hbm, thick), (ocean_hbm, ocean),
            (wind_hbm, wind), (kappa_hbm, kappa), (temp_hbm, temp),
        ])
    ]
    for load in loads:
        load.start()

    barrier = pltpu.get_barrier_semaphore()
    for target in (east, west, partner):
        pl.semaphore_signal(barrier, inc=1, device_id=(ens, target), device_id_type=MESH)

    @pl.when(partner_east != here)
    def _():
        pl.semaphore_signal(barrier, inc=1, device_id=(ens, partner_east), device_id_type=MESH)

    @pl.when(partner_west != here)
    def _():
        pl.semaphore_signal(barrier, inc=1, device_id=(ens, partner_west), device_id_type=MESH)

    for load in loads[:4]:
        load.wait()

    sub = lax.broadcasted_iota(jnp.int32, (8, 128), 0)
    chunks = []
    for start in range(0, n, 8):
        chunk = jnp.zeros((8, 128), jnp.float32)
        for row in range(0, 8, width):
            value = mask[(start + row) // width].astype(jnp.float32)
            chunk = jnp.where(sub >= row, value, chunk)
        chunks.append(chunk)
    weights = jnp.concatenate(chunks, 0)
    weight_ref[...] = weights
    total = area[0]
    volume = area[0] * thick[0]
    for cat in range(1, area.shape[0]):
        total = total + area[cat]
        volume = volume + area[cat] * thick[cat]
    total_ref[...] = total
    half_strength = (13.75 * weights) * volume * jnp.exp(-20.0 * (1.0 - total))
    inner = pl.ds(HALO, n)
    values = []
    for comp in range(2):
        values.append(ocean[comp] * weights)
    for comp in range(2):
        values.append(0.5 * (wind[comp] + ocean[comp]) * weights)
    values.append(half_strength)

    pick_row = lax.broadcasted_iota(jnp.int32, (2 * HALO, 128), 0)
    pick_lane = lax.broadcasted_iota(jnp.int32, (2 * HALO, 128), 1)
    wanted = jnp.where(pick_row < HALO, 128 - HALO + pick_row, 127 + HALO - pick_row)
    pick = jnp.where(pick_lane == wanted, 1.0, 0.0).astype(jnp.float32)
    place_col = lax.broadcasted_iota(jnp.int32, (n, 2 * n), 0)
    place_lane = lax.broadcasted_iota(jnp.int32, (n, 2 * n), 1)
    place_lane = jnp.where(place_lane >= n, place_lane - n, place_lane)
    place = jnp.where(place_lane == place_col, 1.0, 0.0).astype(jnp.float32)
    place_back = jnp.where(n - 1 - place_lane == place_col, 1.0, 0.0).astype(jnp.float32)
    tops = []
    for k in range(FIELDS):
        fields[k, inner, :] = values[k]
        tops.append(lax.dot_general(
            pick, values[k], (((1,), (1,)), ((), ())), precision=HIGH,
            preferred_element_type=jnp.float32))
    forward = jnp.concatenate([top[:HALO] for top in tops], 0)
    backward = jnp.concatenate(
        [(-top[HALO:] if k < 4 else top[HALO:]) for k, top in enumerate(tops)], 0)
    strips[...] = jnp.dot(
        forward, place, precision=HIGH, preferred_element_type=jnp.float32
    ).reshape(FIELDS, HALO, 2 * n)
    mirrored[...] = jnp.dot(
        backward, place_back, precision=HIGH, preferred_element_type=jnp.float32
    ).reshape(FIELDS, HALO, 2 * n)

    others = (partner_east != here).astype(jnp.int32) + (partner_west != here).astype(jnp.int32)
    pl.semaphore_wait(barrier, 3 + others)

    def remote(src, dst, slot, target):
        return pltpu.make_async_remote_copy(
            src_ref=src, dst_ref=dst, send_sem=send_sem.at[slot],
            recv_sem=recv_sem.at[slot], device_id=(ens, target), device_id_type=MESH)

    first, last = pl.ds(HALO, HALO), pl.ds(n, HALO)
    copies = [
        remote(mirrored, arrived.at[2], 2, partner),
        remote(strips, arrived.at[0], 0, east),
        remote(strips, arrived.at[1], 1, west),
        remote(fields.at[:, last, :], fields.at[:, pl.ds(0, HALO), :], 5, east),
        remote(fields.at[:, first, :], fields.at[:, pl.ds(HALO + n, HALO), :], 6, west),
    ]
    to_west = remote(mirrored, arrived.at[3], 3, partner_west)
    to_east = remote(mirrored, arrived.at[4], 4, partner_east)

    @pl.when(partner_west != here)
    def _():
        to_west.start()

    @pl.when(partner_west == here)
    def _():
        arrived[3] = mirrored[...]

    @pl.when(partner_east != here)
    def _():
        to_east.start()

    @pl.when(partner_east == here)
    def _():
        arrived[4] = mirrored[...]

    for copy in copies:
        copy.start()

    for load in loads[4:]:
        load.wait()
    factor = None
    solved = None
    for level in range(levels - 1, -1, -1):
        target = temp[level]
        pivot = 1.0
        if level < levels - 1:
            below = kappa[level]
            pivot = 1.0 + below * (1.0 - factor)
            target = target + below * solved
        if level > 0:
            above = kappa[level - 1]
            inverse = 1.0 / (pivot + above)
            factor = above * inverse
            solved = target * inverse
            if level < levels - 1:
                kappa[level] = carried
            carried = factor
            temp[level] = solved
        else:
            kappa[0] = carried
            inverse = 1.0 / pivot
            first_ref[...] = inverse
            temp[0] = target * inverse

    @pl.when(partner_west != here)
    def _():
        to_west.wait()

    @pl.when(partner_east != here)
    def _():
        to_east.wait()

    for copy in copies:
        copy.wait()

    lane = lax.broadcasted_iota(jnp.int32, (HALO, 2 * n), 1)
    strip = []
    for k in range(FIELDS):
        south = jnp.where(
            lane >= n, strips[k], jnp.where(lane >= n // 2, arrived[0, k], arrived[1, k]))
        north = jnp.where(
            lane >= n, arrived[2, k], jnp.where(lane >= n // 2, arrived[4, k], arrived[3, k]))
        strip.append(jnp.concatenate([south, north], 0))
    u, v, fu, fv, half = strip
    for count in range(ITERS):
        rows_ref[2 * count:2 * count + 1, :] = u[HALO:HALO + 1, :]
        rows_ref[2 * count + 1:2 * count + 2, :] = v[HALO:HALO + 1, :]
        if count < ITERS - 1:
            pairs = [
                [pltpu.roll(w, shift, axis) for w in (u, v)]
                for axis, shift in ((1, 2 * n - 1), (1, 1), (0, 2 * HALO - 1), (0, 1))
            ]
            u, v = advance(u, v, *pairs, fu, fv, half)

    turned = rows_ref[...].T
    crossed = jnp.concatenate([turned[n - HALO:], turned[:HALO]], 0)
    u, v, fu, fv, half = [fields[k] for k in range(FIELDS)]
    for count in range(ITERS):
        if count == 2:
            cut = slice(8, n + 24)
            u, v, fu, fv, half, crossed = [w[cut] for w in (u, v, fu, fv, half, crossed)]
        size = u.shape[0]
        rows = lax.broadcasted_iota(jnp.int32, (size, 128), 1)
        eastern = [pltpu.roll(w, size - 1, 0) for w in (u, v)]
        western = [pltpu.roll(w, 1, 0) for w in (u, v)]
        northern = [
            jnp.where(rows == 127, pltpu.roll(crossed, 127 - 2 * count - comp, 1), pltpu.roll(w, 127, 1))
            for comp, w in enumerate((u, v))
        ]
        southern = [jnp.where(rows == 0, 0.0, pltpu.roll(w, 1, 1)) for w in (u, v)]
        u, v = advance(u, v, eastern, western, northern, southern, fu, fv, half)

    source = jnp.zeros((n, 128), jnp.float32)
    scale = total_ref[...] * weight_ref[...]
    for comp, w in enumerate((u, v)):
        w = w[8:8 + n]
        velocity[comp] = w
        drag = scale * (w - ocean[comp])
        stress[comp] = drag
        source = source + drag * ocean[comp]
    stores = [
        pltpu.make_async_copy(velocity, velocity_hbm, out_sem.at[0]),
        pltpu.make_async_copy(stress, stress_hbm, out_sem.at[1]),
    ]
    for store in stores:
        store.start()
    level_value = temp[0] + first_ref[...] * source
    temp[0] = level_value
    quarter = levels // 4
    for level in range(1, levels):
        level_value = temp[level] + kappa[level - 1] * level_value
        temp[level] = level_value
        if level % quarter == quarter - 1:
            part = pl.ds(level - quarter + 1, quarter)
            store = pltpu.make_async_copy(
                temp.at[part], mixed_hbm.at[part], out_sem.at[2 + level // quarter])
            store.start()
            stores.append(store)
    for store in stores:
        store.wait()


def solution(mesh):
    slots = mesh.shape["gx"]

    def body(ocean_vel, wind_stress, ice_area, ice_thick, block_mask, temp, kappa):
        n, ny = ocean_vel.shape[1:]
        levels, cats = temp.shape[0], ice_area.shape[0]
        any_spec = pl.BlockSpec(memory_space=pl.ANY)
        f32 = jnp.float32
        return pl.pallas_call(
            functools.partial(kernel, slots),
            out_shape=(
                jax.ShapeDtypeStruct(temp.shape, f32),
                jax.ShapeDtypeStruct(ocean_vel.shape, f32),
                jax.ShapeDtypeStruct(ocean_vel.shape, f32),
            ),
            in_specs=[pl.BlockSpec(memory_space=pltpu.SMEM)] + [any_spec] * 6,
            out_specs=(any_spec,) * 3,
            scratch_shapes=[
                pltpu.VMEM((2, n, ny), f32),
                pltpu.VMEM((2, n, ny), f32),
                pltpu.VMEM((cats, n, ny), f32),
                pltpu.VMEM((cats, n, ny), f32),
                pltpu.VMEM((levels, n, ny), f32),
                pltpu.VMEM((levels - 1, n, ny), f32),
                pltpu.VMEM((FIELDS, n + 2 * HALO, ny), f32),
                pltpu.VMEM((FIELDS, HALO, 2 * n), f32),
                pltpu.VMEM((FIELDS, HALO, 2 * n), f32),
                pltpu.VMEM((5, FIELDS, HALO, 2 * n), f32),
                pltpu.VMEM((n, ny), f32),
                pltpu.VMEM((n, ny), f32),
                pltpu.VMEM((n, ny), f32),
                pltpu.VMEM((128, 2 * n), f32),
                pltpu.VMEM((2, n, ny), f32),
                pltpu.VMEM((2, n, ny), f32),
                pltpu.SemaphoreType.DMA((6,)),
                pltpu.SemaphoreType.DMA((6,)),
                pltpu.SemaphoreType.DMA((7,)),
                pltpu.SemaphoreType.DMA((7,)),
            ],
            compiler_params=pltpu.CompilerParams(
                collective_id=0, has_side_effects=True, vmem_limit_bytes=24 * 1024 * 1024),
            name="ice_ocean",
        )(block_mask, ocean_vel, wind_stress, ice_area, ice_thick, temp, kappa)

    split = P("ens", "gx", None)
    return jax.shard_map(
        body,
        mesh=mesh,
        in_specs=(split, split, split, split, P(("ens", "gx")), split, split),
        out_specs=(split, split, split),
        check_vma=False,
    )
```

```python
import functools

import jax
import jax.numpy as jnp
from jax import lax
from jax.experimental import pallas as pl
from jax.experimental.pallas import tpu as pltpu
from jax.sharding import PartitionSpec as P

ITERS = 10
HALO = 16
FIELDS = 5
MESH = pl.DeviceIdType.MESH
HIGH = lax.Precision.HIGHEST


def advance(u, v, eastern, western, northern, southern, fu, fv, half_strength):
    (eu, ev), (wu, wv), (nu, nv), (su, sv) = eastern, western, northern, southern
    du_x = eu - wu
    dv_y = nv - sv
    shear = (nu - su) + (ev - wv)
    plus = du_x + dv_y
    minus = du_x - dv_y
    squared = plus * plus + (4.0 * (minus * minus + shear * shear) + 0.04)
    half_zeta = half_strength * lax.rsqrt(squared)
    scale = 1.0 / (1.5 + 4.0 * half_zeta)
    new_u = (u + half_zeta * ((eu + wu) + (nu + su)) + fu) * scale
    new_v = (v + half_zeta * ((ev + wv) + (nv + sv)) + fv) * scale
    return new_u, new_v


def kernel(
    slots, mask_hbm, ocean_hbm, wind_hbm, area_hbm, thick_hbm, temp_hbm, kappa_hbm,
    mixed_hbm, velocity_hbm, stress_hbm,
    mask, ocean, wind, area, thick, temp, kappa, fields, strips, mirrored, arrived,
    total_ref, weight_ref, first_ref, rows_ref, velocity, stress,
    in_sem, out_sem, send_sem, recv_sem,
):
    n = ocean.shape[1]
    levels = temp.shape[0]
    width = n // mask.shape[0]
    ens, here = lax.axis_index("ens"), lax.axis_index("gx")
    east = lax.rem(here + 1, slots)
    west = lax.rem(here + slots - 1, slots)
    partner = slots - 1 - here
    partner_east = lax.rem(partner + 1, slots)
    partner_west = lax.rem(partner + slots - 1, slots)

    loads = [
        pltpu.make_async_copy(src, dst, in_sem.at[k])
        for k, (src, dst) in enumerate([
            (mask_hbm, mask), (area_hbm, area), (thick_hbm, thick), (ocean_hbm, ocean),
            (wind_hbm, wind), (kappa_hbm, kappa), (temp_hbm, temp),
        ])
    ]
    for load in loads:
        load.start()

    barrier = pltpu.get_barrier_semaphore()
    for target in (east, west, partner):
        pl.semaphore_signal(barrier, inc=1, device_id=(ens, target), device_id_type=MESH)

    @pl.when(partner_east != here)
    def _():
        pl.semaphore_signal(barrier, inc=1, device_id=(ens, partner_east), device_id_type=MESH)

    @pl.when(partner_west != here)
    def _():
        pl.semaphore_signal(barrier, inc=1, device_id=(ens, partner_west), device_id_type=MESH)

    for load in loads[:5]:
        load.wait()

    sub = lax.broadcasted_iota(jnp.int32, (8, 128), 0)
    chunks = []
    for start in range(0, n, 8):
        chunk = jnp.zeros((8, 128), jnp.float32)
        for row in range(0, 8, width):
            value = mask[(start + row) // width].astype(jnp.float32)
            chunk = jnp.where(sub >= row, value, chunk)
        chunks.append(chunk)
    weights = jnp.concatenate(chunks, 0)
    weight_ref[...] = weights
    total = area[0]
    volume = area[0] * thick[0]
    for cat in range(1, area.shape[0]):
        total = total + area[cat]
        volume = volume + area[cat] * thick[cat]
    total_ref[...] = total
    half_strength = (13.75 * weights) * volume * jnp.exp(-20.0 * (1.0 - total))
    inner = pl.ds(HALO, n)
    values = []
    for comp in range(2):
        values.append(ocean[comp] * weights)
    for comp in range(2):
        values.append(0.5 * (wind[comp] + ocean[comp]) * weights)
    values.append(half_strength)

    pick_row = lax.broadcasted_iota(jnp.int32, (2 * HALO, 128), 0)
    pick_lane = lax.broadcasted_iota(jnp.int32, (2 * HALO, 128), 1)
    wanted = jnp.where(pick_row < HALO, 128 - HALO + pick_row, 127 + HALO - pick_row)
    pick = jnp.where(pick_lane == wanted, 1.0, 0.0).astype(jnp.float32)
    place_col = lax.broadcasted_iota(jnp.int32, (n, 2 * n), 0)
    place_lane = lax.broadcasted_iota(jnp.int32, (n, 2 * n), 1)
    place_lane = jnp.where(place_lane >= n, place_lane - n, place_lane)
    place = jnp.where(place_lane == place_col, 1.0, 0.0).astype(jnp.float32)
    place_back = jnp.where(n - 1 - place_lane == place_col, 1.0, 0.0).astype(jnp.float32)
    tops = []
    for k in range(FIELDS):
        fields[k, inner, :] = values[k]
        tops.append(lax.dot_general(
            pick, values[k], (((1,), (1,)), ((), ())), precision=HIGH,
            preferred_element_type=jnp.float32))
    forward = jnp.concatenate([top[:HALO] for top in tops], 0)
    backward = jnp.concatenate(
        [(-top[HALO:] if k < 4 else top[HALO:]) for k, top in enumerate(tops)], 0)
    strips[...] = jnp.dot(
        forward, place, precision=HIGH, preferred_element_type=jnp.float32
    ).reshape(FIELDS, HALO, 2 * n)
    mirrored[...] = jnp.dot(
        backward, place_back, precision=HIGH, preferred_element_type=jnp.float32
    ).reshape(FIELDS, HALO, 2 * n)

    others = (partner_east != here).astype(jnp.int32) + (partner_west != here).astype(jnp.int32)
    pl.semaphore_wait(barrier, 3 + others)

    def remote(src, dst, slot, target):
        return pltpu.make_async_remote_copy(
            src_ref=src, dst_ref=dst, send_sem=send_sem.at[slot],
            recv_sem=recv_sem.at[slot], device_id=(ens, target), device_id_type=MESH)

    first, last = pl.ds(HALO, HALO), pl.ds(n, HALO)
    copies = [
        remote(mirrored, arrived.at[2], 2, partner),
        remote(strips, arrived.at[0], 0, east),
        remote(strips, arrived.at[1], 1, west),
        remote(fields.at[:, last, :], fields.at[:, pl.ds(0, HALO), :], 5, east),
        remote(fields.at[:, first, :], fields.at[:, pl.ds(HALO + n, HALO), :], 6, west),
    ]
    to_west = remote(mirrored, arrived.at[3], 3, partner_west)
    to_east = remote(mirrored, arrived.at[4], 4, partner_east)

    @pl.when(partner_west != here)
    def _():
        to_west.start()

    @pl.when(partner_west == here)
    def _():
        arrived[3] = mirrored[...]

    @pl.when(partner_east != here)
    def _():
        to_east.start()

    @pl.when(partner_east == here)
    def _():
        arrived[4] = mirrored[...]

    for copy in copies:
        copy.start()

    for load in loads[5:]:
        load.wait()
    factor = None
    solved = None
    for level in range(levels - 1, -1, -1):
        target = temp[level]
        pivot = 1.0
        if level < levels - 1:
            below = kappa[level]
            pivot = 1.0 + below * (1.0 - factor)
            target = target + below * solved
        if level > 0:
            above = kappa[level - 1]
            inverse = 1.0 / (pivot + above)
            factor = above * inverse
            solved = target * inverse
            if level < levels - 1:
                kappa[level] = carried
            carried = factor
            temp[level] = solved
        else:
            kappa[0] = carried
            inverse = 1.0 / pivot
            first_ref[...] = inverse
            temp[0] = target * inverse

    @pl.when(partner_west != here)
    def _():
        to_west.wait()

    @pl.when(partner_east != here)
    def _():
        to_east.wait()

    for copy in copies:
        copy.wait()

    lane = lax.broadcasted_iota(jnp.int32, (HALO, 2 * n), 1)
    strip = []
    for k in range(FIELDS):
        south = jnp.where(
            lane >= n, strips[k], jnp.where(lane >= n // 2, arrived[0, k], arrived[1, k]))
        north = jnp.where(
            lane >= n, arrived[2, k], jnp.where(lane >= n // 2, arrived[4, k], arrived[3, k]))
        strip.append(jnp.concatenate([south, north], 0))
    u, v, fu, fv, half = strip
    for count in range(ITERS):
        rows_ref[2 * count:2 * count + 1, :] = u[HALO:HALO + 1, :]
        rows_ref[2 * count + 1:2 * count + 2, :] = v[HALO:HALO + 1, :]
        if count < ITERS - 1:
            pairs = [
                [pltpu.roll(w, shift, axis) for w in (u, v)]
                for axis, shift in ((1, 2 * n - 1), (1, 1), (0, 2 * HALO - 1), (0, 1))
            ]
            u, v = advance(u, v, *pairs, fu, fv, half)

    turned = rows_ref[...].T
    crossed = jnp.concatenate([turned[n - HALO:], turned[:HALO]], 0)
    u, v, fu, fv, half = [fields[k] for k in range(FIELDS)]
    for count in range(ITERS):
        if count == 2:
            cut = slice(8, n + 24)
            u, v, fu, fv, half, crossed = [w[cut] for w in (u, v, fu, fv, half, crossed)]
        size = u.shape[0]
        rows = lax.broadcasted_iota(jnp.int32, (size, 128), 1)
        eastern = [pltpu.roll(w, size - 1, 0) for w in (u, v)]
        western = [pltpu.roll(w, 1, 0) for w in (u, v)]
        northern = [
            jnp.where(rows == 127, pltpu.roll(crossed, 127 - 2 * count - comp, 1), pltpu.roll(w, 127, 1))
            for comp, w in enumerate((u, v))
        ]
        southern = [jnp.where(rows == 0, 0.0, pltpu.roll(w, 1, 1)) for w in (u, v)]
        u, v = advance(u, v, eastern, western, northern, southern, fu, fv, half)

    source = jnp.zeros((n, 128), jnp.float32)
    scale = total_ref[...] * weight_ref[...]
    for comp, w in enumerate((u, v)):
        w = w[8:8 + n]
        velocity[comp] = w
        drag = scale * (w - ocean[comp])
        stress[comp] = drag
        source = source + drag * ocean[comp]
    stores = [
        pltpu.make_async_copy(velocity, velocity_hbm, out_sem.at[0]),
        pltpu.make_async_copy(stress, stress_hbm, out_sem.at[1]),
    ]
    for store in stores:
        store.start()
    level_value = temp[0] + first_ref[...] * source
    temp[0] = level_value
    quarter = levels // 4
    for level in range(1, levels):
        level_value = temp[level] + kappa[level - 1] * level_value
        temp[level] = level_value
        if level % quarter == quarter - 1:
            part = pl.ds(level - quarter + 1, quarter)
            store = pltpu.make_async_copy(
                temp.at[part], mixed_hbm.at[part], out_sem.at[2 + level // quarter])
            store.start()
            stores.append(store)
    for store in stores:
        store.wait()


def solution(mesh):
    slots = mesh.shape["gx"]

    def body(ocean_vel, wind_stress, ice_area, ice_thick, block_mask, temp, kappa):
        n, ny = ocean_vel.shape[1:]
        levels, cats = temp.shape[0], ice_area.shape[0]
        any_spec = pl.BlockSpec(memory_space=pl.ANY)
        f32 = jnp.float32
        return pl.pallas_call(
            functools.partial(kernel, slots),
            out_shape=(
                jax.ShapeDtypeStruct(temp.shape, f32),
                jax.ShapeDtypeStruct(ocean_vel.shape, f32),
                jax.ShapeDtypeStruct(ocean_vel.shape, f32),
            ),
            in_specs=[any_spec] * 7,
            out_specs=(any_spec,) * 3,
            scratch_shapes=[
                pltpu.SMEM(block_mask.shape, jnp.int32),
                pltpu.VMEM((2, n, ny), f32),
                pltpu.VMEM((2, n, ny), f32),
                pltpu.VMEM((cats, n, ny), f32),
                pltpu.VMEM((cats, n, ny), f32),
                pltpu.VMEM((levels, n, ny), f32),
                pltpu.VMEM((levels - 1, n, ny), f32),
                pltpu.VMEM((FIELDS, n + 2 * HALO, ny), f32),
                pltpu.VMEM((FIELDS, HALO, 2 * n), f32),
                pltpu.VMEM((FIELDS, HALO, 2 * n), f32),
                pltpu.VMEM((5, FIELDS, HALO, 2 * n), f32),
                pltpu.VMEM((n, ny), f32),
                pltpu.VMEM((n, ny), f32),
                pltpu.VMEM((n, ny), f32),
                pltpu.VMEM((128, 2 * n), f32),
                pltpu.VMEM((2, n, ny), f32),
                pltpu.VMEM((2, n, ny), f32),
                pltpu.SemaphoreType.DMA((7,)),
                pltpu.SemaphoreType.DMA((6,)),
                pltpu.SemaphoreType.DMA((7,)),
                pltpu.SemaphoreType.DMA((7,)),
            ],
            compiler_params=pltpu.CompilerParams(
                collective_id=0, has_side_effects=True, vmem_limit_bytes=60 * 1024 * 1024),
            name="ice_ocean",
        )(block_mask, ocean_vel, wind_stress, ice_area, ice_thick, temp, kappa)

    split = P("ens", "gx", None)
    return jax.shard_map(
        body,
        mesh=mesh,
        in_specs=(split, split, split, split, P(("ens", "gx")), split, split),
        out_specs=(split, split, split),
        check_vma=False,
    )
```

```python
import functools

import jax
import jax.numpy as jnp
from jax import lax
from jax.experimental import pallas as pl
from jax.experimental.pallas import tpu as pltpu
from jax.sharding import PartitionSpec as P

ITERS = 10
HALO = 16
FIELDS = 5
MESH = pl.DeviceIdType.MESH
HIGH = lax.Precision.HIGHEST


def advance(u, v, eastern, western, northern, southern, fu, fv, half_strength):
    (eu, ev), (wu, wv), (nu, nv), (su, sv) = eastern, western, northern, southern
    du_x = eu - wu
    dv_y = nv - sv
    shear = (nu - su) + (ev - wv)
    plus = du_x + dv_y
    minus = du_x - dv_y
    squared = plus * plus + (4.0 * (minus * minus + shear * shear) + 0.04)
    half_zeta = half_strength * lax.rsqrt(squared)
    scale = 1.0 / (1.5 + 4.0 * half_zeta)
    new_u = (u + half_zeta * ((eu + wu) + (nu + su)) + fu) * scale
    new_v = (v + half_zeta * ((ev + wv) + (nv + sv)) + fv) * scale
    return new_u, new_v


def kernel(
    slots, mask_hbm, ocean_hbm, wind_hbm, area_hbm, thick_hbm, temp_hbm, kappa_hbm,
    result,
    mask, ocean, wind, area, thick, temp, kappa, fields, strips, mirrored, arrived,
    total_ref, weight_ref, first_ref, rows_ref,
    in_sem, send_sem, recv_sem,
):
    n = ocean.shape[1]
    levels = temp.shape[0]
    solved_out = result.at[pl.ds(0, levels)]
    factor_out = result.at[pl.ds(levels, levels - 1)]
    velocity = result.at[pl.ds(2 * levels - 1, 2)]
    stress = result.at[pl.ds(2 * levels + 1, 2)]
    width = n // mask.shape[0]
    ens, here = lax.axis_index("ens"), lax.axis_index("gx")
    east = lax.rem(here + 1, slots)
    west = lax.rem(here + slots - 1, slots)
    partner = slots - 1 - here
    partner_east = lax.rem(partner + 1, slots)
    partner_west = lax.rem(partner + slots - 1, slots)

    loads = [
        pltpu.make_async_copy(src, dst, in_sem.at[k])
        for k, (src, dst) in enumerate([
            (mask_hbm, mask), (area_hbm, area), (thick_hbm, thick), (ocean_hbm, ocean),
            (wind_hbm, wind), (kappa_hbm, kappa), (temp_hbm, temp),
        ])
    ]
    for load in loads:
        load.start()

    barrier = pltpu.get_barrier_semaphore()
    for target in (east, west, partner):
        pl.semaphore_signal(barrier, inc=1, device_id=(ens, target), device_id_type=MESH)

    @pl.when(partner_east != here)
    def _():
        pl.semaphore_signal(barrier, inc=1, device_id=(ens, partner_east), device_id_type=MESH)

    @pl.when(partner_west != here)
    def _():
        pl.semaphore_signal(barrier, inc=1, device_id=(ens, partner_west), device_id_type=MESH)

    for load in loads[:5]:
        load.wait()

    sub = lax.broadcasted_iota(jnp.int32, (8, 128), 0)
    chunks = []
    for start in range(0, n, 8):
        chunk = jnp.zeros((8, 128), jnp.float32)
        for row in range(0, 8, width):
            value = mask[(start + row) // width].astype(jnp.float32)
            chunk = jnp.where(sub >= row, value, chunk)
        chunks.append(chunk)
    weights = jnp.concatenate(chunks, 0)
    weight_ref[...] = weights
    total = area[0]
    volume = area[0] * thick[0]
    for cat in range(1, area.shape[0]):
        total = total + area[cat]
        volume = volume + area[cat] * thick[cat]
    total_ref[...] = total
    half_strength = (13.75 * weights) * volume * jnp.exp(-20.0 * (1.0 - total))
    inner = pl.ds(HALO, n)
    values = []
    for comp in range(2):
        values.append(ocean[comp] * weights)
    for comp in range(2):
        values.append(0.5 * (wind[comp] + ocean[comp]) * weights)
    values.append(half_strength)

    pick_row = lax.broadcasted_iota(jnp.int32, (2 * HALO, 128), 0)
    pick_lane = lax.broadcasted_iota(jnp.int32, (2 * HALO, 128), 1)
    wanted = jnp.where(pick_row < HALO, 128 - HALO + pick_row, 127 + HALO - pick_row)
    pick = jnp.where(pick_lane == wanted, 1.0, 0.0).astype(jnp.float32)
    place_col = lax.broadcasted_iota(jnp.int32, (n, 2 * n), 0)
    place_lane = lax.broadcasted_iota(jnp.int32, (n, 2 * n), 1)
    place_lane = jnp.where(place_lane >= n, place_lane - n, place_lane)
    place = jnp.where(place_lane == place_col, 1.0, 0.0).astype(jnp.float32)
    place_back = jnp.where(n - 1 - place_lane == place_col, 1.0, 0.0).astype(jnp.float32)
    tops = []
    for k in range(FIELDS):
        fields[k, inner, :] = values[k]
        tops.append(lax.dot_general(
            pick, values[k], (((1,), (1,)), ((), ())), precision=HIGH,
            preferred_element_type=jnp.float32))
    forward = jnp.concatenate([top[:HALO] for top in tops], 0)
    backward = jnp.concatenate(
        [(-top[HALO:] if k < 4 else top[HALO:]) for k, top in enumerate(tops)], 0)
    strips[...] = jnp.dot(
        forward, place, precision=HIGH, preferred_element_type=jnp.float32
    ).reshape(FIELDS, HALO, 2 * n)
    mirrored[...] = jnp.dot(
        backward, place_back, precision=HIGH, preferred_element_type=jnp.float32
    ).reshape(FIELDS, HALO, 2 * n)

    others = (partner_east != here).astype(jnp.int32) + (partner_west != here).astype(jnp.int32)
    pl.semaphore_wait(barrier, 3 + others)

    def remote(src, dst, slot, target):
        return pltpu.make_async_remote_copy(
            src_ref=src, dst_ref=dst, send_sem=send_sem.at[slot],
            recv_sem=recv_sem.at[slot], device_id=(ens, target), device_id_type=MESH)

    first, last = pl.ds(HALO, HALO), pl.ds(n, HALO)
    copies = [
        remote(mirrored, arrived.at[2], 2, partner),
        remote(strips, arrived.at[0], 0, east),
        remote(strips, arrived.at[1], 1, west),
        remote(fields.at[:, last, :], fields.at[:, pl.ds(0, HALO), :], 5, east),
        remote(fields.at[:, first, :], fields.at[:, pl.ds(HALO + n, HALO), :], 6, west),
    ]
    to_west = remote(mirrored, arrived.at[3], 3, partner_west)
    to_east = remote(mirrored, arrived.at[4], 4, partner_east)

    @pl.when(partner_west != here)
    def _():
        to_west.start()

    @pl.when(partner_west == here)
    def _():
        arrived[3] = mirrored[...]

    @pl.when(partner_east != here)
    def _():
        to_east.start()

    @pl.when(partner_east == here)
    def _():
        arrived[4] = mirrored[...]

    for copy in copies:
        copy.start()

    for load in loads[5:]:
        load.wait()
    factor = None
    solved = None
    for level in range(levels - 1, -1, -1):
        target = temp[level]
        pivot = 1.0
        if level < levels - 1:
            below = kappa[level]
            pivot = 1.0 + below * (1.0 - factor)
            target = target + below * solved
        if level > 0:
            above = kappa[level - 1]
            inverse = 1.0 / (pivot + above)
            factor = above * inverse
            solved = target * inverse
            if level < levels - 1:
                factor_out[level] = carried
            carried = factor
            solved_out[level] = solved
        else:
            factor_out[0] = carried
            inverse = 1.0 / pivot
            first_ref[...] = inverse
            solved_out[0] = target * inverse

    @pl.when(partner_west != here)
    def _():
        to_west.wait()

    @pl.when(partner_east != here)
    def _():
        to_east.wait()

    for copy in copies:
        copy.wait()

    lane = lax.broadcasted_iota(jnp.int32, (HALO, 2 * n), 1)
    strip = []
    for k in range(FIELDS):
        south = jnp.where(
            lane >= n, strips[k], jnp.where(lane >= n // 2, arrived[0, k], arrived[1, k]))
        north = jnp.where(
            lane >= n, arrived[2, k], jnp.where(lane >= n // 2, arrived[4, k], arrived[3, k]))
        strip.append(jnp.concatenate([south, north], 0))
    u, v, fu, fv, half = strip
    for count in range(ITERS):
        rows_ref[2 * count:2 * count + 1, :] = u[HALO:HALO + 1, :]
        rows_ref[2 * count + 1:2 * count + 2, :] = v[HALO:HALO + 1, :]
        if count < ITERS - 1:
            pairs = [
                [pltpu.roll(w, shift, axis) for w in (u, v)]
                for axis, shift in ((1, 2 * n - 1), (1, 1), (0, 2 * HALO - 1), (0, 1))
            ]
            u, v = advance(u, v, *pairs, fu, fv, half)

    turned = rows_ref[...].T
    crossed = jnp.concatenate([turned[n - HALO:], turned[:HALO]], 0)
    u, v, fu, fv, half = [fields[k] for k in range(FIELDS)]
    for count in range(ITERS):
        if count == 2:
            cut = slice(8, n + 24)
            u, v, fu, fv, half, crossed = [w[cut] for w in (u, v, fu, fv, half, crossed)]
        size = u.shape[0]
        rows = lax.broadcasted_iota(jnp.int32, (size, 128), 1)
        eastern = [pltpu.roll(w, size - 1, 0) for w in (u, v)]
        western = [pltpu.roll(w, 1, 0) for w in (u, v)]
        northern = [
            jnp.where(rows == 127, pltpu.roll(crossed, 127 - 2 * count - comp, 1), pltpu.roll(w, 127, 1))
            for comp, w in enumerate((u, v))
        ]
        southern = [jnp.where(rows == 0, 0.0, pltpu.roll(w, 1, 1)) for w in (u, v)]
        u, v = advance(u, v, eastern, western, northern, southern, fu, fv, half)

    source = jnp.zeros((n, 128), jnp.float32)
    scale = total_ref[...] * weight_ref[...]
    for comp, w in enumerate((u, v)):
        w = w[8:8 + n]
        velocity[comp] = w
        drag = scale * (w - ocean[comp])
        stress[comp] = drag
        source = source + drag * ocean[comp]
    solved_out[0] = solved_out[0] + first_ref[...] * source


def back_kernel(middle, mixed_hbm, velocity_hbm, stress_hbm, mixed, out_sem):
    levels = mixed.shape[0]
    velocity = middle.at[pl.ds(2 * levels - 1, 2)]
    stress = middle.at[pl.ds(2 * levels + 1, 2)]
    stores = [
        pltpu.make_async_copy(velocity, velocity_hbm, out_sem.at[0]),
        pltpu.make_async_copy(stress, stress_hbm, out_sem.at[1]),
    ]
    for store in stores:
        store.start()
    value = middle[0]
    mixed[0] = value
    quarter = levels // 4
    for level in range(1, levels):
        value = middle[level] + middle[levels + level - 1] * value
        mixed[level] = value
        if level % quarter == quarter - 1:
            part = pl.ds(level - quarter + 1, quarter)
            store = pltpu.make_async_copy(
                mixed.at[part], mixed_hbm.at[part], out_sem.at[2 + level // quarter])
            store.start()
            stores.append(store)
    for store in stores:
        store.wait()


def solution(mesh):
    slots = mesh.shape["gx"]

    def body(ocean_vel, wind_stress, ice_area, ice_thick, block_mask, temp, kappa):
        n, ny = ocean_vel.shape[1:]
        levels, cats = temp.shape[0], ice_area.shape[0]
        f32 = jnp.float32
        hbm = pl.BlockSpec(memory_space=pltpu.HBM)
        vmem = pl.BlockSpec(memory_space=pltpu.VMEM)
        column = jax.ShapeDtypeStruct(temp.shape, f32)
        pair = jax.ShapeDtypeStruct(ocean_vel.shape, f32)
        middle = pl.pallas_call(
            functools.partial(kernel, slots),
            out_shape=jax.ShapeDtypeStruct((2 * levels + 3, n, ny), f32),
            in_specs=[hbm] * 7,
            out_specs=vmem,
            scratch_shapes=[
                pltpu.SMEM(block_mask.shape, jnp.int32),
                pltpu.VMEM((2, n, ny), f32),
                pltpu.VMEM((2, n, ny), f32),
                pltpu.VMEM((cats, n, ny), f32),
                pltpu.VMEM((cats, n, ny), f32),
                pltpu.VMEM((levels, n, ny), f32),
                pltpu.VMEM((levels - 1, n, ny), f32),
                pltpu.VMEM((FIELDS, n + 2 * HALO, ny), f32),
                pltpu.VMEM((FIELDS, HALO, 2 * n), f32),
                pltpu.VMEM((FIELDS, HALO, 2 * n), f32),
                pltpu.VMEM((5, FIELDS, HALO, 2 * n), f32),
                pltpu.VMEM((n, ny), f32),
                pltpu.VMEM((n, ny), f32),
                pltpu.VMEM((n, ny), f32),
                pltpu.VMEM((128, 2 * n), f32),
                pltpu.SemaphoreType.DMA((7,)),
                pltpu.SemaphoreType.DMA((7,)),
                pltpu.SemaphoreType.DMA((7,)),
            ],
            compiler_params=pltpu.CompilerParams(
                collective_id=0, has_side_effects=True, vmem_limit_bytes=60817408),
            name="ice_ocean",
        )(block_mask, ocean_vel, wind_stress, ice_area, ice_thick, temp, kappa)
        return pl.pallas_call(
            back_kernel,
            out_shape=(column, pair, pair),
            in_specs=[vmem],
            out_specs=(hbm,) * 3,
            scratch_shapes=[pltpu.VMEM(temp.shape, f32), pltpu.SemaphoreType.DMA((6,))],
            compiler_params=pltpu.CompilerParams(vmem_limit_bytes=10 * 1024 * 1024),
            name="back_substitution",
        )(middle)

    split = P("ens", "gx", None)
    return jax.shard_map(
        body,
        mesh=mesh,
        in_specs=(split, split, split, split, P(("ens", "gx")), split, split),
        out_specs=(split, split, split),
        check_vma=False,
    )
```

```python
import functools

import jax
import jax.numpy as jnp
from jax import lax
from jax.experimental import pallas as pl
from jax.experimental.pallas import tpu as pltpu
from jax.sharding import PartitionSpec as P

ITERS = 10
HALO = 16
FIELDS = 5
MESH = pl.DeviceIdType.MESH
HIGH = lax.Precision.HIGHEST


def advance(u, v, eastern, western, northern, southern, fu, fv, half_strength):
    (eu, ev), (wu, wv), (nu, nv), (su, sv) = eastern, western, northern, southern
    du_x = eu - wu
    dv_y = nv - sv
    shear = (nu - su) + (ev - wv)
    plus = du_x + dv_y
    minus = du_x - dv_y
    squared = plus * plus + (4.0 * (minus * minus + shear * shear) + 0.04)
    half_zeta = half_strength * lax.rsqrt(squared)
    scale = 1.0 / (1.5 + 4.0 * half_zeta)
    new_u = (u + half_zeta * ((eu + wu) + (nu + su)) + fu) * scale
    new_v = (v + half_zeta * ((ev + wv) + (nv + sv)) + fv) * scale
    return new_u, new_v


def kernel(
    slots, mask_hbm, ocean_hbm, wind_hbm, area_hbm, thick_hbm, temp_hbm, kappa_hbm,
    result,
    mask, ocean, wind, area, thick, temp, kappa, fields, strips, mirrored, arrived, packed, corners,
    total_ref, weight_ref, first_ref, rows_ref,
    in_sem, send_sem, recv_sem,
):
    n = ocean.shape[1]
    levels = temp.shape[0]
    solved_out = result.at[pl.ds(0, levels)]
    factor_out = result.at[pl.ds(levels, levels - 1)]
    velocity = result.at[pl.ds(2 * levels - 1, 2)]
    stress = result.at[pl.ds(2 * levels + 1, 2)]
    width = n // mask.shape[0]
    ens, here = lax.axis_index("ens"), lax.axis_index("gx")
    east = lax.rem(here + 1, slots)
    west = lax.rem(here + slots - 1, slots)
    partner = slots - 1 - here
    partner_east = lax.rem(partner + 1, slots)
    partner_west = lax.rem(partner + slots - 1, slots)

    loads = [
        pltpu.make_async_copy(src, dst, in_sem.at[k])
        for k, (src, dst) in enumerate([
            (mask_hbm, mask), (area_hbm, area), (thick_hbm, thick), (ocean_hbm, ocean),
            (wind_hbm, wind), (kappa_hbm, kappa), (temp_hbm, temp),
        ])
    ]
    for load in loads:
        load.start()

    barrier = pltpu.get_barrier_semaphore()
    for target in (east, west, partner):
        pl.semaphore_signal(barrier, inc=1, device_id=(ens, target), device_id_type=MESH)

    @pl.when(partner_east != here)
    def _():
        pl.semaphore_signal(barrier, inc=1, device_id=(ens, partner_east), device_id_type=MESH)

    @pl.when(partner_west != here)
    def _():
        pl.semaphore_signal(barrier, inc=1, device_id=(ens, partner_west), device_id_type=MESH)

    for load in loads[:5]:
        load.wait()

    sub = lax.broadcasted_iota(jnp.int32, (8, 128), 0)
    chunks = []
    for start in range(0, n, 8):
        chunk = jnp.zeros((8, 128), jnp.float32)
        for row in range(0, 8, width):
            value = mask[(start + row) // width].astype(jnp.float32)
            chunk = jnp.where(sub >= row, value, chunk)
        chunks.append(chunk)
    weights = jnp.concatenate(chunks, 0)
    weight_ref[...] = weights
    total = area[0]
    volume = area[0] * thick[0]
    for cat in range(1, area.shape[0]):
        total = total + area[cat]
        volume = volume + area[cat] * thick[cat]
    total_ref[...] = total
    half_strength = (13.75 * weights) * volume * jnp.exp(-20.0 * (1.0 - total))
    inner = pl.ds(HALO, n)
    values = []
    for comp in range(2):
        values.append(ocean[comp] * weights)
    for comp in range(2):
        values.append(0.5 * (wind[comp] + ocean[comp]) * weights)
    values.append(half_strength)

    pick_row = lax.broadcasted_iota(jnp.int32, (2 * HALO, 128), 0)
    pick_lane = lax.broadcasted_iota(jnp.int32, (2 * HALO, 128), 1)
    wanted = jnp.where(pick_row < HALO, 128 - HALO + pick_row, 127 + HALO - pick_row)
    pick = jnp.where(pick_lane == wanted, 1.0, 0.0).astype(jnp.float32)
    place_col = lax.broadcasted_iota(jnp.int32, (n, 2 * n), 0)
    place_lane = lax.broadcasted_iota(jnp.int32, (n, 2 * n), 1)
    place_lane = jnp.where(place_lane >= n, place_lane - n, place_lane)
    place = jnp.where(place_lane == place_col, 1.0, 0.0).astype(jnp.float32)
    place_back = jnp.where(n - 1 - place_lane == place_col, 1.0, 0.0).astype(jnp.float32)
    tops = []
    for k in range(FIELDS):
        fields[k, inner, :] = values[k]
        tops.append(lax.dot_general(
            pick, values[k], (((1,), (1,)), ((), ())), precision=HIGH,
            preferred_element_type=jnp.float32))
    forward = jnp.concatenate([top[:HALO] for top in tops], 0)
    backward = jnp.concatenate(
        [(-top[HALO:] if k < 4 else top[HALO:]) for k, top in enumerate(tops)], 0)
    plain = jnp.dot(forward, place, precision=HIGH, preferred_element_type=jnp.float32)
    plain = plain.reshape(FIELDS, HALO, 2 * n)
    strips[...] = plain
    turned = jnp.dot(backward, place_back, precision=HIGH, preferred_element_type=jnp.float32)
    turned = turned.reshape(FIELDS, HALO, 2 * n)
    mirrored[...] = turned
    slot = lax.broadcasted_iota(jnp.int32, (HALO, 128), 1)
    for index, (block, base) in enumerate(
        [(plain, 0), (plain, n - HALO), (turned, 0), (turned, n - HALO)]
    ):
        tile = jnp.zeros((HALO, 128), jnp.float32)
        for k in range(FIELDS):
            shift = (HALO * k - base) % (2 * n)
            moved = pltpu.roll(block[k], shift, 1) if shift else block[k]
            tile = jnp.where(slot >= HALO * k, moved[:, :128], tile)
        packed[index] = tile

    others = (partner_east != here).astype(jnp.int32) + (partner_west != here).astype(jnp.int32)
    pl.semaphore_wait(barrier, 3 + others)

    def remote(src, dst, slot, target):
        return pltpu.make_async_remote_copy(
            src_ref=src, dst_ref=dst, send_sem=send_sem.at[slot],
            recv_sem=recv_sem.at[slot], device_id=(ens, target), device_id_type=MESH)

    first, last = pl.ds(HALO, HALO), pl.ds(n, HALO)
    copies = [
        remote(mirrored, arrived, 2, partner),
        remote(packed.at[1], corners.at[1], 0, east),
        remote(packed.at[0], corners.at[0], 1, west),
        remote(fields.at[:, last, :], fields.at[:, pl.ds(0, HALO), :], 5, east),
        remote(fields.at[:, first, :], fields.at[:, pl.ds(HALO + n, HALO), :], 6, west),
    ]
    to_west = remote(packed.at[2], corners.at[2], 3, partner_west)
    to_east = remote(packed.at[3], corners.at[3], 4, partner_east)

    @pl.when(partner_west != here)
    def _():
        to_west.start()

    @pl.when(partner_west == here)
    def _():
        corners[2] = packed[2]

    @pl.when(partner_east != here)
    def _():
        to_east.start()

    @pl.when(partner_east == here)
    def _():
        corners[3] = packed[3]

    for copy in copies:
        copy.start()

    for load in loads[5:]:
        load.wait()
    factor = None
    solved = None
    for level in range(levels - 1, -1, -1):
        target = temp[level]
        pivot = 1.0
        if level < levels - 1:
            below = kappa[level]
            pivot = 1.0 + below * (1.0 - factor)
            target = target + below * solved
        if level > 0:
            above = kappa[level - 1]
            inverse = 1.0 / (pivot + above)
            factor = above * inverse
            solved = target * inverse
            if level < levels - 1:
                factor_out[level] = carried
            carried = factor
            solved_out[level] = solved
        else:
            factor_out[0] = carried
            inverse = 1.0 / pivot
            first_ref[...] = inverse
            solved_out[0] = target * inverse

    @pl.when(partner_west != here)
    def _():
        to_west.wait()

    @pl.when(partner_east != here)
    def _():
        to_east.wait()

    for copy in copies:
        copy.wait()

    lane = lax.broadcasted_iota(jnp.int32, (HALO, 2 * n), 1)
    tiles = []
    for index in range(4):
        tile = corners[index]
        if 2 * n > 128:
            tile = jnp.concatenate([tile, jnp.zeros((HALO, 2 * n - 128), jnp.float32)], 1)
        tiles.append(tile)

    def unpack(index, base, k):
        shift = (base - HALO * k) % (2 * n)
        return pltpu.roll(tiles[index], shift, 1) if shift else tiles[index]

    strip = []
    for k in range(FIELDS):
        low, high, low_turned, high_turned = [
            unpack(index, (index % 2) * (n - HALO), k) for index in range(4)]
        south = jnp.where(lane >= n, strips[k], jnp.where(lane >= n // 2, high, low))
        north = jnp.where(
            lane >= n, arrived[k], jnp.where(lane >= n // 2, high_turned, low_turned))
        strip.append(jnp.concatenate([south, north], 0))
    u, v, fu, fv, half = strip
    for count in range(ITERS):
        rows_ref[2 * count:2 * count + 1, :] = u[HALO:HALO + 1, :]
        rows_ref[2 * count + 1:2 * count + 2, :] = v[HALO:HALO + 1, :]
        if count < ITERS - 1:
            pairs = [
                [pltpu.roll(w, shift, axis) for w in (u, v)]
                for axis, shift in ((1, 2 * n - 1), (1, 1), (0, 2 * HALO - 1), (0, 1))
            ]
            u, v = advance(u, v, *pairs, fu, fv, half)

    turned = rows_ref[...].T
    crossed = jnp.concatenate([turned[n - HALO:], turned[:HALO]], 0)
    u, v, fu, fv, half = [fields[k] for k in range(FIELDS)]
    for count in range(ITERS):
        if count == 2:
            cut = slice(8, n + 24)
            u, v, fu, fv, half, crossed = [w[cut] for w in (u, v, fu, fv, half, crossed)]
        size = u.shape[0]
        rows = lax.broadcasted_iota(jnp.int32, (size, 128), 1)
        eastern = [pltpu.roll(w, size - 1, 0) for w in (u, v)]
        western = [pltpu.roll(w, 1, 0) for w in (u, v)]
        northern = [
            jnp.where(rows == 127, pltpu.roll(crossed, 127 - 2 * count - comp, 1), pltpu.roll(w, 127, 1))
            for comp, w in enumerate((u, v))
        ]
        southern = [jnp.where(rows == 0, 0.0, pltpu.roll(w, 1, 1)) for w in (u, v)]
        u, v = advance(u, v, eastern, western, northern, southern, fu, fv, half)

    source = jnp.zeros((n, 128), jnp.float32)
    scale = total_ref[...] * weight_ref[...]
    for comp, w in enumerate((u, v)):
        w = w[8:8 + n]
        velocity[comp] = w
        drag = scale * (w - ocean[comp])
        stress[comp] = drag
        source = source + drag * ocean[comp]
    solved_out[0] = solved_out[0] + first_ref[...] * source


def back_kernel(middle, mixed_hbm, velocity_hbm, stress_hbm, mixed, out_sem):
    levels = mixed.shape[0]
    velocity = middle.at[pl.ds(2 * levels - 1, 2)]
    stress = middle.at[pl.ds(2 * levels + 1, 2)]
    stores = [
        pltpu.make_async_copy(velocity, velocity_hbm, out_sem.at[0]),
        pltpu.make_async_copy(stress, stress_hbm, out_sem.at[1]),
    ]
    for store in stores:
        store.start()
    value = middle[0]
    mixed[0] = value
    quarter = levels // 4
    for level in range(1, levels):
        value = middle[level] + middle[levels + level - 1] * value
        mixed[level] = value
        if level % quarter == quarter - 1:
            part = pl.ds(level - quarter + 1, quarter)
            store = pltpu.make_async_copy(
                mixed.at[part], mixed_hbm.at[part], out_sem.at[2 + level // quarter])
            store.start()
            stores.append(store)
    for store in stores:
        store.wait()


def solution(mesh):
    slots = mesh.shape["gx"]

    def body(ocean_vel, wind_stress, ice_area, ice_thick, block_mask, temp, kappa):
        n, ny = ocean_vel.shape[1:]
        levels, cats = temp.shape[0], ice_area.shape[0]
        f32 = jnp.float32
        hbm = pl.BlockSpec(memory_space=pltpu.HBM)
        vmem = pl.BlockSpec(memory_space=pltpu.VMEM)
        column = jax.ShapeDtypeStruct(temp.shape, f32)
        pair = jax.ShapeDtypeStruct(ocean_vel.shape, f32)
        middle = pl.pallas_call(
            functools.partial(kernel, slots),
            out_shape=jax.ShapeDtypeStruct((2 * levels + 3, n, ny), f32),
            in_specs=[hbm] * 7,
            out_specs=vmem,
            scratch_shapes=[
                pltpu.SMEM(block_mask.shape, jnp.int32),
                pltpu.VMEM((2, n, ny), f32),
                pltpu.VMEM((2, n, ny), f32),
                pltpu.VMEM((cats, n, ny), f32),
                pltpu.VMEM((cats, n, ny), f32),
                pltpu.VMEM((levels, n, ny), f32),
                pltpu.VMEM((levels - 1, n, ny), f32),
                pltpu.VMEM((FIELDS, n + 2 * HALO, ny), f32),
                pltpu.VMEM((FIELDS, HALO, 2 * n), f32),
                pltpu.VMEM((FIELDS, HALO, 2 * n), f32),
                pltpu.VMEM((FIELDS, HALO, 2 * n), f32),
                pltpu.VMEM((4, HALO, 128), f32),
                pltpu.VMEM((4, HALO, 128), f32),
                pltpu.VMEM((n, ny), f32),
                pltpu.VMEM((n, ny), f32),
                pltpu.VMEM((n, ny), f32),
                pltpu.VMEM((128, 2 * n), f32),
                pltpu.SemaphoreType.DMA((7,)),
                pltpu.SemaphoreType.DMA((7,)),
                pltpu.SemaphoreType.DMA((7,)),
            ],
            compiler_params=pltpu.CompilerParams(
                collective_id=0, has_side_effects=True, vmem_limit_bytes=60817408),
            name="ice_ocean",
        )(block_mask, ocean_vel, wind_stress, ice_area, ice_thick, temp, kappa)
        return pl.pallas_call(
            back_kernel,
            out_shape=(column, pair, pair),
            in_specs=[vmem],
            out_specs=(hbm,) * 3,
            scratch_shapes=[pltpu.VMEM(temp.shape, f32), pltpu.SemaphoreType.DMA((6,))],
            compiler_params=pltpu.CompilerParams(vmem_limit_bytes=10 * 1024 * 1024),
            name="back_substitution",
        )(middle)

    split = P("ens", "gx", None)
    return jax.shard_map(
        body,
        mesh=mesh,
        in_specs=(split, split, split, split, P(("ens", "gx")), split, split),
        out_specs=(split, split, split),
        check_vma=False,
    )
```

```python
import functools

import jax
import jax.numpy as jnp
from jax import lax
from jax.experimental import pallas as pl
from jax.experimental.pallas import tpu as pltpu
from jax.sharding import PartitionSpec as P

ITERS = 10
HALO = 16
FIELDS = 5
MESH = pl.DeviceIdType.MESH
HIGH = lax.Precision.HIGHEST


def advance(u, v, eastern, western, northern, southern, fu, fv, half_strength):
    (eu, ev), (wu, wv), (nu, nv), (su, sv) = eastern, western, northern, southern
    du_x = eu - wu
    dv_y = nv - sv
    shear = (nu - su) + (ev - wv)
    plus = du_x + dv_y
    minus = du_x - dv_y
    squared = plus * plus + (4.0 * (minus * minus + shear * shear) + 0.04)
    half_zeta = half_strength * lax.rsqrt(squared)
    scale = 1.0 / (1.5 + 4.0 * half_zeta)
    new_u = (u + half_zeta * ((eu + wu) + (nu + su)) + fu) * scale
    new_v = (v + half_zeta * ((ev + wv) + (nv + sv)) + fv) * scale
    return new_u, new_v


def kernel(
    slots, mask_hbm, ocean_hbm, wind_hbm, area_hbm, thick_hbm, temp_hbm, kappa_hbm,
    result,
    mask, ocean, wind, area, thick, temp, kappa, fields, strips, mirrored, arrived, packed, corners,
    total_ref, weight_ref, first_ref, rows_ref,
    in_sem, send_sem, recv_sem,
):
    n = ocean.shape[1]
    levels = temp.shape[0]
    solved_out = result.at[pl.ds(0, levels)]
    factor_out = result.at[pl.ds(levels, levels - 1)]
    velocity = result.at[pl.ds(2 * levels - 1, 2)]
    stress = result.at[pl.ds(2 * levels + 1, 2)]
    width = n // mask.shape[0]
    ens, here = lax.axis_index("ens"), lax.axis_index("gx")
    east = lax.rem(here + 1, slots)
    west = lax.rem(here + slots - 1, slots)
    partner = slots - 1 - here
    partner_east = lax.rem(partner + 1, slots)
    partner_west = lax.rem(partner + slots - 1, slots)

    loads = [
        pltpu.make_async_copy(src, dst, in_sem.at[k])
        for k, (src, dst) in enumerate([
            (mask_hbm, mask), (area_hbm, area), (thick_hbm, thick), (ocean_hbm, ocean),
            (wind_hbm, wind), (kappa_hbm, kappa), (temp_hbm, temp),
        ])
    ]
    for load in loads:
        load.start()

    barrier = pltpu.get_barrier_semaphore()
    for target in (east, west, partner):
        pl.semaphore_signal(barrier, inc=1, device_id=(ens, target), device_id_type=MESH)

    @pl.when(partner_east != here)
    def _():
        pl.semaphore_signal(barrier, inc=1, device_id=(ens, partner_east), device_id_type=MESH)

    @pl.when(partner_west != here)
    def _():
        pl.semaphore_signal(barrier, inc=1, device_id=(ens, partner_west), device_id_type=MESH)

    for load in loads[:5]:
        load.wait()

    sub = lax.broadcasted_iota(jnp.int32, (8, 128), 0)
    chunks = []
    for start in range(0, n, 8):
        chunk = jnp.zeros((8, 128), jnp.float32)
        for row in range(0, 8, width):
            value = mask[(start + row) // width].astype(jnp.float32)
            chunk = jnp.where(sub >= row, value, chunk)
        chunks.append(chunk)
    weights = jnp.concatenate(chunks, 0)
    weight_ref[...] = weights
    total = area[0]
    volume = area[0] * thick[0]
    for cat in range(1, area.shape[0]):
        total = total + area[cat]
        volume = volume + area[cat] * thick[cat]
    total_ref[...] = total
    half_strength = (13.75 * weights) * volume * jnp.exp(-20.0 * (1.0 - total))
    inner = pl.ds(HALO, n)
    values = []
    for comp in range(2):
        values.append(ocean[comp] * weights)
    for comp in range(2):
        values.append(0.5 * (wind[comp] + ocean[comp]) * weights)
    values.append(half_strength)

    pick_row = lax.broadcasted_iota(jnp.int32, (2 * HALO, 128), 0)
    pick_lane = lax.broadcasted_iota(jnp.int32, (2 * HALO, 128), 1)
    wanted = jnp.where(pick_row < HALO, 128 - HALO + pick_row, 127 + HALO - pick_row)
    pick = jnp.where(pick_lane == wanted, 1.0, 0.0).astype(jnp.float32)
    place_col = lax.broadcasted_iota(jnp.int32, (n, 2 * n), 0)
    place_lane = lax.broadcasted_iota(jnp.int32, (n, 2 * n), 1)
    place_lane = jnp.where(place_lane >= n, place_lane - n, place_lane)
    place = jnp.where(place_lane == place_col, 1.0, 0.0).astype(jnp.float32)
    place_back = jnp.where(n - 1 - place_lane == place_col, 1.0, 0.0).astype(jnp.float32)
    tops = []
    for k in range(FIELDS):
        fields[k, inner, :] = values[k]
        tops.append(lax.dot_general(
            pick, values[k], (((1,), (1,)), ((), ())), precision=HIGH,
            preferred_element_type=jnp.float32))
    forward = jnp.concatenate([top[:HALO] for top in tops], 0)
    backward = jnp.concatenate(
        [(-top[HALO:] if k < 4 else top[HALO:]) for k, top in enumerate(tops)], 0)
    plain = jnp.dot(forward, place, precision=HIGH, preferred_element_type=jnp.float32)
    plain = plain.reshape(FIELDS, HALO, 2 * n)
    strips[...] = plain
    turned = jnp.dot(backward, place_back, precision=HIGH, preferred_element_type=jnp.float32)
    turned = turned.reshape(FIELDS, HALO, 2 * n)
    half_lane = lax.broadcasted_iota(jnp.int32, (HALO, 2 * n), 1)
    for pair in range(3):
        mirrored[pair] = jnp.where(
            half_lane < n, turned[2 * pair], turned[min(2 * pair + 1, FIELDS - 1)])
    slot = lax.broadcasted_iota(jnp.int32, (HALO, 128), 1)
    for index, (block, base) in enumerate(
        [(plain, 0), (plain, n - HALO), (turned, 0), (turned, n - HALO)]
    ):
        tile = jnp.zeros((HALO, 128), jnp.float32)
        for k in range(FIELDS):
            shift = (HALO * k - base) % (2 * n)
            moved = pltpu.roll(block[k], shift, 1) if shift else block[k]
            tile = jnp.where(slot >= HALO * k, moved[:, :128], tile)
        packed[index] = tile

    others = (partner_east != here).astype(jnp.int32) + (partner_west != here).astype(jnp.int32)
    pl.semaphore_wait(barrier, 3 + others)

    def remote(src, dst, slot, target):
        return pltpu.make_async_remote_copy(
            src_ref=src, dst_ref=dst, send_sem=send_sem.at[slot],
            recv_sem=recv_sem.at[slot], device_id=(ens, target), device_id_type=MESH)

    first, last = pl.ds(HALO, HALO), pl.ds(n, HALO)
    copies = [
        remote(mirrored, arrived, 2, partner),
        remote(packed.at[1], corners.at[1], 0, east),
        remote(packed.at[0], corners.at[0], 1, west),
        remote(fields.at[:, last, :], fields.at[:, pl.ds(0, HALO), :], 5, east),
        remote(fields.at[:, first, :], fields.at[:, pl.ds(HALO + n, HALO), :], 6, west),
    ]
    to_west = remote(packed.at[2], corners.at[2], 3, partner_west)
    to_east = remote(packed.at[3], corners.at[3], 4, partner_east)

    @pl.when(partner_west != here)
    def _():
        to_west.start()

    @pl.when(partner_west == here)
    def _():
        corners[2] = packed[2]

    @pl.when(partner_east != here)
    def _():
        to_east.start()

    @pl.when(partner_east == here)
    def _():
        corners[3] = packed[3]

    for copy in copies:
        copy.start()

    for load in loads[5:]:
        load.wait()
    factor = None
    solved = None
    for level in range(levels - 1, -1, -1):
        target = temp[level]
        pivot = 1.0
        if level < levels - 1:
            below = kappa[level]
            pivot = 1.0 + below * (1.0 - factor)
            target = target + below * solved
        if level > 0:
            above = kappa[level - 1]
            inverse = 1.0 / (pivot + above)
            factor = above * inverse
            solved = target * inverse
            if level < levels - 1:
                factor_out[level] = carried
            carried = factor
            solved_out[level] = solved
        else:
            factor_out[0] = carried
            inverse = 1.0 / pivot
            first_ref[...] = inverse
            solved_out[0] = target * inverse

    @pl.when(partner_west != here)
    def _():
        to_west.wait()

    @pl.when(partner_east != here)
    def _():
        to_east.wait()

    for copy in copies:
        copy.wait()

    lane = lax.broadcasted_iota(jnp.int32, (HALO, 2 * n), 1)
    tiles = []
    for index in range(4):
        tile = corners[index]
        if 2 * n > 128:
            tile = jnp.concatenate([tile, jnp.zeros((HALO, 2 * n - 128), jnp.float32)], 1)
        tiles.append(tile)

    def unpack(index, base, k):
        shift = (base - HALO * k) % (2 * n)
        return pltpu.roll(tiles[index], shift, 1) if shift else tiles[index]

    strip = []
    for k in range(FIELDS):
        low, high, low_turned, high_turned = [
            unpack(index, (index % 2) * (n - HALO), k) for index in range(4)]
        opposite = arrived[k // 2]
        if k % 2 == 0 and k < FIELDS - 1:
            opposite = pltpu.roll(opposite, n, 1)
        south = jnp.where(lane >= n, strips[k], jnp.where(lane >= n // 2, high, low))
        north = jnp.where(
            lane >= n, opposite, jnp.where(lane >= n // 2, high_turned, low_turned))
        strip.append(jnp.concatenate([south, north], 0))
    u, v, fu, fv, half = strip
    for count in range(ITERS):
        rows_ref[2 * count:2 * count + 1, :] = u[HALO:HALO + 1, :]
        rows_ref[2 * count + 1:2 * count + 2, :] = v[HALO:HALO + 1, :]
        if count < ITERS - 1:
            pairs = [
                [pltpu.roll(w, shift, axis) for w in (u, v)]
                for axis, shift in ((1, 2 * n - 1), (1, 1), (0, 2 * HALO - 1), (0, 1))
            ]
            u, v = advance(u, v, *pairs, fu, fv, half)

    turned = rows_ref[...].T
    crossed = jnp.concatenate([turned[n - HALO:], turned[:HALO]], 0)
    u, v, fu, fv, half = [fields[k] for k in range(FIELDS)]
    for count in range(ITERS):
        if count == 2:
            cut = slice(8, n + 24)
            u, v, fu, fv, half, crossed = [w[cut] for w in (u, v, fu, fv, half, crossed)]
        size = u.shape[0]
        rows = lax.broadcasted_iota(jnp.int32, (size, 128), 1)
        eastern = [pltpu.roll(w, size - 1, 0) for w in (u, v)]
        western = [pltpu.roll(w, 1, 0) for w in (u, v)]
        northern = [
            jnp.where(rows == 127, pltpu.roll(crossed, 127 - 2 * count - comp, 1), pltpu.roll(w, 127, 1))
            for comp, w in enumerate((u, v))
        ]
        southern = [jnp.where(rows == 0, 0.0, pltpu.roll(w, 1, 1)) for w in (u, v)]
        u, v = advance(u, v, eastern, western, northern, southern, fu, fv, half)

    source = jnp.zeros((n, 128), jnp.float32)
    scale = total_ref[...] * weight_ref[...]
    for comp, w in enumerate((u, v)):
        w = w[8:8 + n]
        velocity[comp] = w
        drag = scale * (w - ocean[comp])
        stress[comp] = drag
        source = source + drag * ocean[comp]
    solved_out[0] = solved_out[0] + first_ref[...] * source


def back_kernel(middle, mixed_hbm, velocity_hbm, stress_hbm, mixed, out_sem):
    levels = mixed.shape[0]
    velocity = middle.at[pl.ds(2 * levels - 1, 2)]
    stress = middle.at[pl.ds(2 * levels + 1, 2)]
    stores = [
        pltpu.make_async_copy(velocity, velocity_hbm, out_sem.at[0]),
        pltpu.make_async_copy(stress, stress_hbm, out_sem.at[1]),
    ]
    for store in stores:
        store.start()
    value = middle[0]
    mixed[0] = value
    quarter = levels // 4
    for level in range(1, levels):
        value = middle[level] + middle[levels + level - 1] * value
        mixed[level] = value
        if level % quarter == quarter - 1:
            part = pl.ds(level - quarter + 1, quarter)
            store = pltpu.make_async_copy(
                mixed.at[part], mixed_hbm.at[part], out_sem.at[2 + level // quarter])
            store.start()
            stores.append(store)
    for store in stores:
        store.wait()


def solution(mesh):
    slots = mesh.shape["gx"]

    def body(ocean_vel, wind_stress, ice_area, ice_thick, block_mask, temp, kappa):
        n, ny = ocean_vel.shape[1:]
        levels, cats = temp.shape[0], ice_area.shape[0]
        f32 = jnp.float32
        hbm = pl.BlockSpec(memory_space=pltpu.HBM)
        vmem = pl.BlockSpec(memory_space=pltpu.VMEM)
        column = jax.ShapeDtypeStruct(temp.shape, f32)
        pair = jax.ShapeDtypeStruct(ocean_vel.shape, f32)
        middle = pl.pallas_call(
            functools.partial(kernel, slots),
            out_shape=jax.ShapeDtypeStruct((2 * levels + 3, n, ny), f32),
            in_specs=[hbm] * 7,
            out_specs=vmem,
            scratch_shapes=[
                pltpu.SMEM(block_mask.shape, jnp.int32),
                pltpu.VMEM((2, n, ny), f32),
                pltpu.VMEM((2, n, ny), f32),
                pltpu.VMEM((cats, n, ny), f32),
                pltpu.VMEM((cats, n, ny), f32),
                pltpu.VMEM((levels, n, ny), f32),
                pltpu.VMEM((levels - 1, n, ny), f32),
                pltpu.VMEM((FIELDS, n + 2 * HALO, ny), f32),
                pltpu.VMEM((FIELDS, HALO, 2 * n), f32),
                pltpu.VMEM((3, HALO, 2 * n), f32),
                pltpu.VMEM((3, HALO, 2 * n), f32),
                pltpu.VMEM((4, HALO, 128), f32),
                pltpu.VMEM((4, HALO, 128), f32),
                pltpu.VMEM((n, ny), f32),
                pltpu.VMEM((n, ny), f32),
                pltpu.VMEM((n, ny), f32),
                pltpu.VMEM((128, 2 * n), f32),
                pltpu.SemaphoreType.DMA((7,)),
                pltpu.SemaphoreType.DMA((7,)),
                pltpu.SemaphoreType.DMA((7,)),
            ],
            compiler_params=pltpu.CompilerParams(
                collective_id=0, has_side_effects=True, vmem_limit_bytes=60817408),
            name="ice_ocean",
        )(block_mask, ocean_vel, wind_stress, ice_area, ice_thick, temp, kappa)
        return pl.pallas_call(
            back_kernel,
            out_shape=(column, pair, pair),
            in_specs=[vmem],
            out_specs=(hbm,) * 3,
            scratch_shapes=[pltpu.VMEM(temp.shape, f32), pltpu.SemaphoreType.DMA((6,))],
            compiler_params=pltpu.CompilerParams(vmem_limit_bytes=10 * 1024 * 1024),
            name="back_substitution",
        )(middle)

    split = P("ens", "gx", None)
    return jax.shard_map(
        body,
        mesh=mesh,
        in_specs=(split, split, split, split, P(("ens", "gx")), split, split),
        out_specs=(split, split, split),
        check_vma=False,
    )
```
